128 devices in a mesh: table: 16 (over z, x), pre: 8 (over y, core).
Axes of the slice: x: 4, y: 4, z: 4, core: 2. Of those that a mesh axis runs over, the one named last changes fastest.
Arguments:
- table: bfloat16 [1024, 512, 512], P('table', 'pre'), may hold values from -6 to 6
- grads: bfloat16 [256, 512, 512], P('table', 'pre'), may hold values from -68 to 68
- left_stats: float32 [128, 512, 512], P(('table', 'pre')), as said below
- right_stats: float32 [128, 512, 512], P(('table', 'pre')), as said below
- block_ids: int32 [16, 16], P('table'), may hold values from -1 to 63, as said below
- owner_slot: int32 [16, 16], P('table'), may hold values from -1 to 127, as said below
- owner_source: int32 [128], replicated, may hold values from 0 to 15, as said below
Outputs:
- new_table: bfloat16 [1024, 512, 512], P('table', 'pre')
- new_left: float32 [128, 512, 512], P(('table', 'pre'))
- new_right: float32 [128, 512, 512], P(('table', 'pre'))
The draws below stay inside these ranges and needn't reach their ends.
Inputs may be any that keep to these rules, and one draw needn't show every extreme that they name: `owner_slot`: each owner slot q (device index along table+pre times 1 plus k) appears exactly once in the whole array; a table group sends at most one block to each group of 8 devices that share a table index (q // 8); live slots come first in each row, -1 marks the empty ones; some group has all 16 slots live. `block_ids`: live slots of a row name distinct blocks; -1 exactly where owner_slot is -1. owner_source[q] is the row of owner_slot that holds q. `left_stats`: Symmetric; each diagonal entry exceeds the summed magnitudes of the rest of its row. `right_stats`: Symmetric; each diagonal entry exceeds the summed magnitudes of the rest of its row.
All inputs are finite; a program needn't handle non-finite values.
Results may differ from the reference program's by a relative error of at most 0.0014.
Values may be sent and summed in bfloat16 or wider, within the bound.
No kernel may reach another device: no remote copies, remote signals or barrier semaphores. Data moves between devices by JAX's collectives and lax.ppermute only.
A program may use at most 128 MiB of HBM per device.

```python
import jax
import jax.numpy as jnp
from jax import lax

WIDTH = 512
BLOCK = 512
SHARD_BLOCKS = 64
OWN = 1
ITERS = 3
MOST = 16
BLOCKS = 1024
N_TABLE = 16
N_PRE = 8


def routing(key):
    groups = N_TABLE
    per_group = N_PRE * OWN
    total = groups * per_group
    keys = jax.random.split(key, 7)
    rows = jnp.arange(groups, dtype=jnp.int32)
    weight = jax.random.randint(keys[0], (groups,), 0, 4)
    star = jax.random.randint(keys[1], (), 0, groups)
    noise = jax.random.randint(keys[2], (groups, groups), 0, 64)
    score = (weight[:, None] * 64 + noise) * groups + rows[:, None]
    score = score + (rows == star).astype(jnp.int32)[:, None] * (1000 * groups)
    column = jax.random.randint(keys[6], (), 0, groups)
    columns_all = jnp.arange(groups, dtype=jnp.int32)
    lifted = (rows[:, None] == groups - 1) & (columns_all[None, :] == column)
    score = score + lifted.astype(jnp.int32) * (500 * groups)
    chosen = lax.top_k(score.T, per_group)[1].astype(jnp.int32)
    shuffle_key = jax.random.randint(keys[3], (groups, per_group), 0, 1000) * per_group + jnp.arange(per_group, dtype=jnp.int32)[None, :]
    order = jnp.argsort(shuffle_key, axis=1)
    chosen = jnp.take_along_axis(chosen, order, axis=1)
    owner_source = chosen.reshape(total).astype(jnp.int32)
    live = owner_source[None, :] == rows[:, None]
    columns = jnp.arange(total, dtype=jnp.int32)[None, :]
    rank_key = jnp.where(live, jax.random.randint(keys[4], (groups, total), 0, 1000) * total + columns, 1000 * total + columns)
    picks = jnp.argsort(rank_key, axis=1)[:, :groups].astype(jnp.int32)
    has = jnp.take_along_axis(live, picks, axis=1)
    owner_slot = jnp.where(has, picks, -1).astype(jnp.int32)

    def pick_blocks(row_key):
        first, second = jax.random.split(row_key)
        base = jax.random.permutation(first, SHARD_BLOCKS - 1)[:groups - 1]
        full = jnp.concatenate([base, jnp.full((1,), SHARD_BLOCKS - 1, base.dtype)])
        return jax.random.permutation(second, full).astype(jnp.int32)
    ids = jax.vmap(pick_blocks)(jax.random.split(keys[5], groups))
    block_ids = jnp.where(has, ids, -1).astype(jnp.int32)
    return (owner_slot, block_ids, owner_source)


def draw_owner_slot(key, part):
    return routing(key)[0]


def draw_block_ids(key, part):
    return routing(key)[1]


def draw_owner_source(key, part):
    return routing(key)[2]


def statistic(key, count, order):
    first, second = jax.random.split(key)
    diag = jnp.exp(jax.random.uniform(first, (count, order), jnp.float32, jnp.log(100.0), jnp.log(1000.0)))
    noise = jax.random.uniform(second, (count, order, order), jnp.float32, -1.0, 1.0)
    noise = 0.5 * (noise + jnp.transpose(noise, (0, 2, 1)))
    root = jnp.sqrt(diag)
    off = 0.2 * noise * root[:, :, None] * root[:, None, :] / order
    ident = jnp.eye(order, dtype=jnp.float32)[None, :, :]
    return off * (1.0 - ident) + ident * diag[:, :, None]


def draw_left_stats(key, part):
    key = jax.random.fold_in(key, 11)
    return statistic(key, N_TABLE * N_PRE * OWN, BLOCK)


def draw_right_stats(key, part):
    key = jax.random.fold_in(key, 12)
    return statistic(key, N_TABLE * N_PRE * OWN, WIDTH)


def draw_grads(key, part):
    key = jax.random.fold_in(key, 5)
    keys = jax.random.split(key, 3)
    count = N_TABLE * MOST
    base = jnp.clip(jax.random.normal(keys[0], (count, BLOCK, WIDTH), jnp.float32), -4.0, 4.0)
    top = jnp.log(4.0)
    rows = jnp.exp(jax.random.uniform(keys[1], (count, BLOCK, 1), jnp.float32, jnp.log(0.5), top))
    cols = jnp.exp(jax.random.uniform(keys[2], (count, 1, WIDTH), jnp.float32, jnp.log(0.5), top))
    return (base * rows * cols).astype(jnp.bfloat16)


def block_levels(stream_key, shape, cuts, low, high):
    loudness = 1.0
    for axis_at, parts in cuts:
        draws = jax.random.uniform(jax.random.fold_in(jax.random.fold_in(stream_key, 6), axis_at), (parts,), jnp.float32, low / len(cuts), high / len(cuts))
        loudness = loudness * jnp.repeat(jnp.exp(draws), shape[axis_at] // parts).reshape((-1,) + (1,) * (len(shape) - 1 - axis_at))
    return loudness


def scatter_about(rng, extent, spread, most, pieces=(), kind=jnp.bfloat16):
    entries = spread * jax.random.normal(rng, extent, jnp.float32)
    if pieces:
        entries = entries * block_levels(rng, extent, pieces, -0.22, 0.18)
    return jnp.clip(entries, -most, most).astype(kind)


def setup_inputs(seed: int = 0) -> dict:
    splits = jax.random.split(jax.random.key(seed), 8)
    return {
        "table": scatter_about(splits[0], (BLOCKS, BLOCK, WIDTH), 1.0, 6.0, ((0, 16), (1, 8))),
        "grads": draw_grads(jax.random.fold_in(splits[7], 71), 0),
        "left_stats": draw_left_stats(jax.random.fold_in(splits[7], 71), 0),
        "right_stats": draw_right_stats(jax.random.fold_in(splits[7], 71), 0),
        "block_ids": draw_block_ids(jax.random.fold_in(splits[7], 71), 0),
        "owner_slot": draw_owner_slot(jax.random.fold_in(splits[7], 71), 0),
        "owner_source": draw_owner_source(jax.random.fold_in(splits[7], 71), 0),
    }


BETA = 0.95
EPSILON = 1.0
RATE = 0.1

def hdot(left, right):
    return jnp.dot(left, right, precision=lax.Precision.HIGHEST, preferred_element_type=jnp.float32)

def inverse_root(stat):
    ident = jnp.eye(stat.shape[0], dtype=jnp.float32)
    shifted = stat + EPSILON * ident
    scale = 2.5 / jnp.sqrt(jnp.sum(shifted * shifted))
    mat_m = shifted * scale
    mat_h = ident * jnp.sqrt(jnp.sqrt(scale))
    for step in range(ITERS):
        factor = (5.0 * ident - mat_m) * 0.25
        mat_h = hdot(mat_h, factor)
        if step + 1 < ITERS:
            square = hdot(factor, factor)
            mat_m = hdot(hdot(square, square), mat_m)
    return mat_h

def shampoo_block(grad, left_old, right_old):
    gram_left = lax.dot_general(grad, grad, (((1,), (1,)), ((), ())), preferred_element_type=jnp.float32)
    gram_right = lax.dot_general(grad, grad, (((0,), (0,)), ((), ())), preferred_element_type=jnp.float32)
    left_new = BETA * left_old + (1.0 - BETA) * gram_left
    right_new = BETA * right_old + (1.0 - BETA) * gram_right
    root_left = inverse_root(left_new)
    root_right = inverse_root(right_new)
    dense = grad.astype(jnp.float32)
    precond = hdot(hdot(root_left, dense), root_right)
    ratio = jnp.sqrt(jnp.sum(dense * dense)) / jnp.sqrt(jnp.sum(precond * precond) + 1e-06)
    return ((precond * ratio).astype(jnp.bfloat16), left_new, right_new)

def reference(table, grads, left_stats, right_stats, block_ids, owner_slot, owner_source):
    slot_index = jnp.arange(owner_slot.shape[1], dtype=jnp.int32)

    def handle(index):
        group = owner_source[index].astype(jnp.int32)
        row = lax.dynamic_index_in_dim(owner_slot, group, 0, keepdims=False)
        ids_row = lax.dynamic_index_in_dim(block_ids, group, 0, keepdims=False)
        slot = jnp.sum(jnp.where(row == index, slot_index, 0)).astype(jnp.int32)
        grad = lax.dynamic_index_in_dim(grads, (group * MOST + slot).astype(jnp.int32), 0, keepdims=False)
        target = (group * SHARD_BLOCKS + jnp.sum(jnp.where(slot_index == slot, ids_row, 0))).astype(jnp.int32)
        left_old = lax.dynamic_index_in_dim(left_stats, index, 0, keepdims=False)
        right_old = lax.dynamic_index_in_dim(right_stats, index, 0, keepdims=False)
        update, left_new, right_new = shampoo_block(grad, left_old, right_old)
        return (update, left_new, right_new, target)
    updates, lefts, rights, targets = lax.map(handle, jnp.arange(owner_source.shape[0], dtype=jnp.int32))
    rows = table[targets].astype(jnp.float32) - RATE * updates.astype(jnp.float32)
    new_table = table.at[targets].set(rows.astype(jnp.bfloat16))
    return (new_table, lefts, rights)
```

```python
import functools

import jax
import jax.numpy as jnp
from jax import lax
from jax.experimental import pallas as pl
from jax.experimental.pallas import tpu as pltpu
from jax.sharding import PartitionSpec as P

BETA = 0.95
EPSILON = 1.0
RATE = 0.1

VMEM = pl.BlockSpec(memory_space=pltpu.VMEM)
SMEM = pl.BlockSpec(memory_space=pltpu.SMEM)
HBM = pl.BlockSpec(memory_space=pl.ANY)


def params():
    return pltpu.CompilerParams(vmem_limit_bytes=48 * 1024 * 1024)


def pack_kernel(n_pre, slots_ref, grads_ref, out_ref, sems):
    capacity = grads_ref.shape[0]

    def copy(j):
        group = lax.div(jnp.maximum(slots_ref[0, j], 0), n_pre)
        return pltpu.make_async_copy(grads_ref.at[j], out_ref.at[group], sems.at[j])

    for j in range(capacity):
        @pl.when(slots_ref[0, j] >= 0)
        def _():
            copy(j).start()
    for j in range(capacity):
        @pl.when(slots_ref[0, j] >= 0)
        def _():
            copy(j).wait()


def pick_kernel(source_ref, got_ref, out_ref, sems):
    n_pre = out_ref.shape[0]
    base = lax.axis_index("table") * n_pre
    copies = [
        pltpu.make_async_copy(got_ref.at[source_ref[base + k]], out_ref.at[k], sems.at[k])
        for k in range(n_pre)
    ]
    for copy in copies:
        copy.start()
    for copy in copies:
        copy.wait()


def spread_kernel(source_ref, got_ref, out_ref, sems):
    n_pre = got_ref.shape[0]
    base = lax.axis_index("table") * n_pre
    copies = [
        pltpu.make_async_copy(got_ref.at[k], out_ref.at[source_ref[base + k]], sems.at[k])
        for k in range(n_pre)
    ]
    for copy in copies:
        copy.start()
    for copy in copies:
        copy.wait()


def apply_kernel(n_pre, slots_ref, ids_ref, table_ref, got_ref, copied_ref, out_ref, held, in_sems, out_sems):
    capacity = slots_ref.shape[1]

    def load(j):
        return pltpu.make_async_copy(
            table_ref.at[jnp.maximum(ids_ref[0, j], 0)], held.at[j], in_sems.at[j]
        )

    def store(j):
        return pltpu.make_async_copy(
            held.at[j], out_ref.at[jnp.maximum(ids_ref[0, j], 0)], out_sems.at[j]
        )

    for j in range(capacity):
        @pl.when(slots_ref[0, j] >= 0)
        def _():
            load(j).start()
    for j in range(capacity):
        @pl.when(slots_ref[0, j] >= 0)
        def _():
            load(j).wait()
            update = got_ref[lax.div(slots_ref[0, j], n_pre)]
            new = held[j].astype(jnp.float32) - RATE * update.astype(jnp.float32)
            held[j] = new.astype(held.dtype)
            store(j).start()
    for j in range(capacity):
        @pl.when(slots_ref[0, j] >= 0)
        def _():
            store(j).wait()


def split(x):
    high = x.astype(jnp.bfloat16)
    return high, (x - high.astype(jnp.float32)).astype(jnp.bfloat16)


def mm(a, b):
    return jnp.dot(a, b, preferred_element_type=jnp.float32)


def mm3(a, b):
    ah, al = a
    bh, bl = b
    return mm(ah, bh) + (mm(al, bh) + mm(ah, bl))


def total(x):
    return jnp.sum(jnp.sum(x, axis=1, keepdims=True), axis=0, keepdims=True)


def root(stat, diagonal):
    order = stat.shape[0]
    shifted = jnp.where(diagonal, stat + EPSILON, stat)
    z = 2.5 / jnp.sqrt(total(shifted * shifted))
    mean = total(jnp.where(diagonal, shifted, 0.0)) * z * (1.0 / order)
    x = jnp.where(diagonal, shifted * z - mean, shifted * z) * 0.25
    k = 1.25 - 0.25 * mean
    xs = split(x)
    y = mm3(xs, xs) - (2.0 * k) * x
    ys = split(y)
    k2 = k * k
    k4 = k2 * k2
    w = mm3(ys, ys) + (2.0 * k2) * y
    x2 = mm3(split(w), xs) + (0.25 * mean) * w + k4 * x
    c = 1.25 - 0.25 * (k4 * mean)
    c2 = c * c
    x2s = split(x2)
    y2 = mm3(x2s, x2s) - (2.0 * c) * x2
    v = c * y2 - c2 * x2 - mm3(split(y2), x2s)
    c3 = c2 * c
    d = c3 - 1.25 * c2
    u = v - 1.25 * y2
    h = mm3(split(v), split(u)) + c3 * u + d * v - 1.25 * x2
    g = 1.25 * c + c3 * d
    return k * g, k * h - g * x - mm3(xs, split(h)), jnp.sqrt(jnp.sqrt(z))


def owner_kernel(grad_ref, left_ref, right_ref, table_ref, update_ref, new_left_ref, new_right_ref, copied_ref, sem):
    copy = pltpu.make_async_copy(table_ref, copied_ref, sem)
    copy.start()
    grad = grad_ref[...]
    order = grad.shape[0]
    rows = lax.broadcasted_iota(jnp.int32, (order, order), 0)
    diagonal = rows == lax.broadcasted_iota(jnp.int32, (order, order), 1)
    gram_left = lax.dot_general(
        grad, grad, (((1,), (1,)), ((), ())), preferred_element_type=jnp.float32
    )
    gram_right = lax.dot_general(
        grad, grad, (((0,), (0,)), ((), ())), preferred_element_type=jnp.float32
    )
    new_left = BETA * left_ref[0] + (1.0 - BETA) * gram_left
    new_right = BETA * right_ref[0] + (1.0 - BETA) * gram_right
    new_left_ref[0] = new_left
    new_right_ref[0] = new_right
    left_one, left_rest, left_scale = root(new_left, diagonal)
    right_one, right_rest, right_scale = root(new_right, diagonal)
    dense = grad.astype(jnp.float32)
    high, low = split(left_rest)
    half = left_one * dense + (mm(high, grad) + mm(low, grad))
    pre = right_one * half + mm3(split(half), split(right_rest))
    scale = left_scale * right_scale
    size = scale * scale * total(pre * pre) + 1e-06
    ratio = scale * jnp.sqrt(total(dense * dense)) / jnp.sqrt(size)
    update_ref[...] = (pre * ratio).astype(update_ref.dtype)
    copy.wait()


def body(table, grads, left_stats, right_stats, block_ids, owner_slot, owner_source):
    n_table = lax.axis_size("table")
    n_pre = lax.axis_size("pre")
    capacity, piece, width = grads.shape
    order = piece * n_pre

    def dma(count):
        return pltpu.SemaphoreType.DMA((count,))

    def shape(*dims):
        return jax.ShapeDtypeStruct(dims, jnp.bfloat16)

    outgoing = pl.pallas_call(
        functools.partial(pack_kernel, n_pre),
        out_shape=shape(n_table, piece, width),
        in_specs=[SMEM, HBM],
        out_specs=VMEM,
        scratch_shapes=[dma(capacity)],
        compiler_params=params(),
    )(owner_slot, grads)
    arrived = lax.all_to_all(outgoing, "table", split_axis=0, concat_axis=0, tiled=True)
    picked = pl.pallas_call(
        pick_kernel,
        out_shape=shape(n_pre, piece, width),
        in_specs=[SMEM, VMEM],
        out_specs=VMEM,
        scratch_shapes=[dma(n_pre)],
        compiler_params=params(),
    )(owner_source, arrived)
    block = lax.all_to_all(picked, "pre", split_axis=0, concat_axis=0, tiled=True)
    update, new_left, new_right, copied = pl.pallas_call(
        owner_kernel,
        out_shape=(
            shape(order, width),
            jax.ShapeDtypeStruct(left_stats.shape, jnp.float32),
            jax.ShapeDtypeStruct(right_stats.shape, jnp.float32),
            jax.ShapeDtypeStruct(table.shape, table.dtype),
        ),
        in_specs=[VMEM, VMEM, VMEM, HBM],
        out_specs=(VMEM, VMEM, VMEM, HBM),
        scratch_shapes=[pltpu.SemaphoreType.DMA],
        compiler_params=params(),
    )(block.reshape(order, width), left_stats, right_stats, table)
    returned = lax.all_to_all(
        update.reshape(n_pre, piece, width), "pre", split_axis=0, concat_axis=0, tiled=True
    )
    spread = pl.pallas_call(
        spread_kernel,
        out_shape=shape(n_table, piece, width),
        in_specs=[SMEM, VMEM],
        out_specs=VMEM,
        scratch_shapes=[dma(n_pre)],
        compiler_params=params(),
    )(owner_source, returned)
    home = lax.all_to_all(spread, "table", split_axis=0, concat_axis=0, tiled=True)
    new_table = pl.pallas_call(
        functools.partial(apply_kernel, n_pre),
        out_shape=jax.ShapeDtypeStruct(table.shape, table.dtype),
        in_specs=[SMEM, SMEM, HBM, VMEM, HBM],
        out_specs=HBM,
        scratch_shapes=[
            pltpu.VMEM((capacity, piece, width), jnp.bfloat16),
            dma(capacity),
            dma(capacity),
        ],
        input_output_aliases={4: 0},
        compiler_params=params(),
    )(owner_slot, block_ids, table, home, copied)
    return (new_table, new_left, new_right)


def solution(mesh):
    placed = (
        P("table", "pre", None),
        P("table", "pre", None),
        P(("table", "pre"), None, None),
        P(("table", "pre"), None, None),
        P("table", None),
        P("table", None),
        P(),
    )
    return jax.shard_map(
        body,
        mesh=mesh,
        in_specs=placed,
        out_specs=(
            P("table", "pre", None),
            P(("table", "pre"), None, None),
            P(("table", "pre"), None, None),
        ),
        check_vma=False,
    )
```

```python
import functools

import jax
import jax.numpy as jnp
from jax import lax
from jax.experimental import pallas as pl
from jax.experimental.pallas import tpu as pltpu
from jax.sharding import PartitionSpec as P

BETA = 0.95
EPSILON = 1.0
RATE = 0.1

VMEM = pl.BlockSpec(memory_space=pltpu.VMEM)
SMEM = pl.BlockSpec(memory_space=pltpu.SMEM)
HBM = pl.BlockSpec(memory_space=pltpu.HBM)


def params(mebibytes):
    return pltpu.CompilerParams(vmem_limit_bytes=mebibytes * 1024 * 1024)


def pack_kernel(n_pre, slots_ref, grads_ref, out_ref):
    for j in range(grads_ref.shape[0]):
        @pl.when(slots_ref[0, j] >= 0)
        def _():
            out_ref[lax.div(slots_ref[0, j], n_pre)] = grads_ref[j]


def pick_kernel(source_ref, got_ref, out_ref):
    n_pre = out_ref.shape[0]
    base = lax.axis_index("table") * n_pre
    for k in range(n_pre):
        out_ref[k] = got_ref[source_ref[base + k]]


def spread_kernel(source_ref, got_ref, out_ref):
    n_pre = got_ref.shape[0]
    base = lax.axis_index("table") * n_pre
    for k in range(n_pre):
        out_ref[source_ref[base + k]] = got_ref[k]


def apply_kernel(n_pre, slots_ref, ids_ref, table_ref, got_ref, copied_ref, out_ref, held, sems):
    capacity = slots_ref.shape[1]

    def store(j):
        return pltpu.make_async_copy(
            held.at[j], out_ref.at[jnp.maximum(ids_ref[0, j], 0)], sems.at[j]
        )

    for j in range(capacity):
        @pl.when(slots_ref[0, j] >= 0)
        def _():
            update = got_ref[lax.div(slots_ref[0, j], n_pre)].astype(jnp.float32)
            new = table_ref[ids_ref[0, j]].astype(jnp.float32) - RATE * update
            held[j] = new.astype(held.dtype)
            store(j).start()
    for j in range(capacity):
        @pl.when(slots_ref[0, j] >= 0)
        def _():
            store(j).wait()


TILE = 128
SIDES = (0, 1)
SMALL = 0.008


def low(x):
    return x.astype(jnp.bfloat16)


def wide(x):
    return x.astype(jnp.float32)


def split(x):
    high = low(x)
    return high, low(x - wide(high))


def mm(a, b):
    return jnp.dot(a, b, preferred_element_type=jnp.float32)


def mm3(a, b):
    ah, al = a
    bh, bl = b
    return mm(ah, bh) + (mm(al, bh) + mm(ah, bl))


def total(x):
    return jnp.sum(jnp.sum(x, axis=0, keepdims=True), axis=1, keepdims=True)


def coefficients(k, mean):
    k4 = (k * k) * (k * k)
    c = 1.25 - 0.25 * (k4 * mean)
    c2 = c * c
    c3 = c2 * c
    d = c3 - 1.25 * c2
    return k4, c, c2, c3, d, 1.25 * c + c3 * d


def careful_root(x, k, mean):
    k4, c, c2, c3, d, g = coefficients(k, mean)
    xs = split(x)
    y = mm3(xs, xs) - (2.0 * k) * x
    ys = split(y)
    w = mm3(ys, ys) + (2.0 * k * k) * y
    x2 = mm3(split(w), xs) + (0.25 * mean) * w + k4 * x
    x2s = split(x2)
    y2 = mm3(x2s, x2s) - (2.0 * c) * x2
    v = c * y2 - c2 * x2 - mm3(split(y2), x2s)
    u = v - 1.25 * y2
    h = mm3(split(v), split(u)) + c3 * u + d * v - 1.25 * x2
    return k * g, k * h - g * x - mm3(xs, split(h))


def owner_kernel(
    grad_ref, left_ref, right_ref, table_ref,
    update_ref, new_left_ref, new_right_ref, copied_ref,
    x, y, e, x2, y2, xh, yh, wh, x2h, y2h, vh, uh, hh, lo, sem,
):
    copy = pltpu.make_async_copy(table_ref, copied_ref, sem)
    copy.start()
    order = grad_ref.shape[0]
    olds, news = (left_ref, right_ref), (new_left_ref, new_right_ref)
    eye = lax.broadcasted_iota(jnp.int32, (TILE, TILE), 0) == lax.broadcasted_iota(
        jnp.int32, (TILE, TILE), 1
    )
    tiles = [pl.ds(at, TILE) for at in range(0, order, TILE)]

    def trace(ref):
        parts = [jnp.where(eye, ref[0, t, t], 0.0) for t in tiles]
        return total(functools.reduce(jnp.add, parts))

    sizes = []
    for s, contract in zip(SIDES, (1, 0)):
        gram = lax.dot_general(
            grad_ref[...], grad_ref[...], (((contract,), (contract,)), ((), ())),
            preferred_element_type=jnp.float32,
        )
        new = BETA * olds[s][0] + (1.0 - BETA) * gram
        news[s][0] = new
        sizes.append(total(new * new))
    dense = wide(grad_ref[...])
    grad_size = total(dense * dense)
    zs, means, ks, coefs = [], [], [], []
    for s in SIDES:
        diag = trace(news[s])
        z = 2.5 / jnp.sqrt(sizes[s] + (2.0 * EPSILON) * diag + EPSILON * EPSILON * order)
        mean = (diag + EPSILON * order) * z * (1.0 / order)
        zs.append(z)
        means.append(mean)
        ks.append(1.25 - 0.25 * mean)
        coefs.append(coefficients(ks[s], mean))
    for s in SIDES:
        scale = 0.25 * zs[s]
        scaled = news[s][0] * scale
        x[s] = scaled
        xh[s] = low(scaled)
        for t in tiles:
            part = news[s][0, t, t] * scale + jnp.where(eye, EPSILON * scale - 0.25 * means[s], 0.0)
            x[s, t, t] = part
            xh[s, t, t] = low(part)

    fourths = []
    for s in SIDES:
        square = mm(xh[s], xh[s])
        fourths.append(total(square * square))
        new = square - (2.0 * ks[s]) * x[s]
        y[s] = new
        yh[s] = low(new)
    small = jnp.sum(jnp.maximum(fourths[0], fourths[1])) <= SMALL
    for s in SIDES:
        wh[s] = low(mm(yh[s], yh[s]) + (2.0 * ks[s] * ks[s]) * y[s])
    for s in SIDES:
        k4 = coefs[s][0]
        new = mm(wh[s], xh[s]) + (0.25 * means[s]) * wide(wh[s]) + k4 * x[s]
        x2[s] = new
        x2h[s] = low(new)

    def finish(left_one, right_one):
        half = left_one * wide(grad_ref[...]) + (mm(vh[0], grad_ref[...]) + mm(lo[0], grad_ref[...]))
        y[0] = half
        yh[0] = low(half)
        yh[1] = low(half - wide(yh[0]))
        pre = right_one * y[0] + (mm(yh[0], vh[1]) + (mm(yh[1], vh[1]) + mm(yh[0], lo[1])))
        y[1] = pre
        scale = jnp.sqrt(jnp.sqrt(zs[0])) * jnp.sqrt(jnp.sqrt(zs[1]))
        size = scale * scale * total(pre * pre) + 1e-06
        ratio = scale * jnp.sqrt(grad_size) / jnp.sqrt(size)
        update_ref[...] = low(y[1] * ratio)

    @pl.when(small)
    def _():
        for s in SIDES:
            c = coefs[s][1]
            new = mm(x2h[s], x2h[s]) - (2.0 * c) * x2[s]
            y2[s] = new
            y2h[s] = low(new)
        for s in SIDES:
            _, c, c2, c3, d, _ = coefs[s]
            square, linear = y2[s], x2[s]
            cube = c * square - c2 * linear - mm(y2h[s], x2h[s])
            rest = cube - 1.25 * square
            vh[s] = low(cube)
            uh[s] = low(rest)
            e[s] = c3 * rest + d * cube - 1.25 * linear
        for s in SIDES:
            g = coefs[s][5]
            new = mm(vh[s], uh[s]) + e[s]
            hh[s] = low(new)
            e[s] = ks[s] * new - g * x[s]
        for s in SIDES:
            new = e[s] - mm(xh[s], hh[s])
            vh[s] = low(new)
            lo[s] = low(new - wide(vh[s]))
        finish(ks[0] * coefs[0][5], ks[1] * coefs[1][5])

    @pl.when(jnp.logical_not(small))
    def _():
        ones = []
        for s in SIDES:
            one, rest = careful_root(x[s], ks[s], means[s])
            ones.append(one)
            vh[s], lo[s] = split(rest)
        finish(*ones)

    copy.wait()


def body(table, grads, left_stats, right_stats, block_ids, owner_slot, owner_source):
    n_table = lax.axis_size("table")
    n_pre = lax.axis_size("pre")
    capacity, piece, width = grads.shape
    order = piece * n_pre

    def shape(*dims):
        return jax.ShapeDtypeStruct(dims, jnp.bfloat16)

    outgoing = pl.pallas_call(
        functools.partial(pack_kernel, n_pre),
        out_shape=shape(n_table, piece, width),
        in_specs=[SMEM, VMEM],
        out_specs=VMEM,
        compiler_params=params(4),
        name="pack",
    )(owner_slot, grads)
    arrived = lax.all_to_all(outgoing, "table", split_axis=0, concat_axis=0, tiled=True)
    picked = pl.pallas_call(
        pick_kernel,
        out_shape=shape(n_pre, piece, width),
        in_specs=[SMEM, VMEM],
        out_specs=VMEM,
        compiler_params=params(4),
        name="pick",
    )(owner_source, arrived)
    block = lax.all_to_all(picked, "pre", split_axis=0, concat_axis=0, tiled=True)
    floats = pltpu.VMEM((2, order, width), jnp.float32)
    halves = pltpu.VMEM((2, order, width), jnp.bfloat16)
    update, new_left, new_right, copied = pl.pallas_call(
        owner_kernel,
        out_shape=(
            shape(order, width),
            jax.ShapeDtypeStruct(left_stats.shape, jnp.float32),
            jax.ShapeDtypeStruct(right_stats.shape, jnp.float32),
            jax.ShapeDtypeStruct(table.shape, table.dtype),
        ),
        in_specs=[VMEM, VMEM, VMEM, VMEM],
        out_specs=(VMEM, VMEM, VMEM, HBM),
        scratch_shapes=[floats] * 5 + [halves] * 9 + [pltpu.SemaphoreType.DMA],
        compiler_params=params(40),
        name="owner",
    )(block.reshape(order, width), left_stats, right_stats, table)
    returned = lax.all_to_all(
        update.reshape(n_pre, piece, width), "pre", split_axis=0, concat_axis=0, tiled=True
    )
    spread = pl.pallas_call(
        spread_kernel,
        out_shape=shape(n_table, piece, width),
        in_specs=[SMEM, VMEM],
        out_specs=VMEM,
        compiler_params=params(4),
        name="spread",
    )(owner_source, returned)
    home = lax.all_to_all(spread, "table", split_axis=0, concat_axis=0, tiled=True)
    new_table = pl.pallas_call(
        functools.partial(apply_kernel, n_pre),
        out_shape=jax.ShapeDtypeStruct(table.shape, table.dtype),
        in_specs=[SMEM, SMEM, VMEM, VMEM, HBM],
        out_specs=HBM,
        scratch_shapes=[
            pltpu.VMEM((capacity, piece, width), jnp.bfloat16),
            pltpu.SemaphoreType.DMA((capacity,)),
        ],
        input_output_aliases={4: 0},
        compiler_params=params(8),
        name="apply",
    )(owner_slot, block_ids, table, home, copied)
    return (new_table, new_left, new_right)


def solution(mesh):
    placed = (
        P("table", "pre", None),
        P("table", "pre", None),
        P(("table", "pre"), None, None),
        P(("table", "pre"), None, None),
        P("table", None),
        P("table", None),
        P(),
    )
    return jax.shard_map(
        body,
        mesh=mesh,
        in_specs=placed,
        out_specs=(
            P("table", "pre", None),
            P(("table", "pre"), None, None),
            P(("table", "pre"), None, None),
        ),
        check_vma=False,
    )
```

```python
import functools

import jax
import jax.numpy as jnp
from jax import lax
from jax.experimental import pallas as pl
from jax.experimental.pallas import tpu as pltpu
from jax.sharding import PartitionSpec as P

BETA = 0.95
EPSILON = 1.0
RATE = 0.1

VMEM = pl.BlockSpec(memory_space=pltpu.VMEM)
SMEM = pl.BlockSpec(memory_space=pltpu.SMEM)
HBM = pl.BlockSpec(memory_space=pltpu.HBM)


def params(mebibytes):
    return pltpu.CompilerParams(vmem_limit_bytes=mebibytes * 1024 * 1024)


class Lists:
    def __init__(self, ref, capacity):
        self.ref, self.capacity = ref, capacity
        self.total = ref.shape[1] - 2 * capacity

    def source(self, owner):
        return self.ref[0, owner]

    def live(self, j):
        return self.ref[0, self.total + j] >= 0

    def group(self, j):
        return lax.div(jnp.maximum(self.ref[0, self.total + j], 0), lax.axis_size("pre"))

    def block(self, j):
        return jnp.maximum(self.ref[0, self.total + self.capacity + j], 0)


def pack_kernel(lists_ref, grads_ref, out_ref):
    capacity = grads_ref.shape[0]
    lists = Lists(lists_ref, capacity)
    for j in range(capacity):
        @pl.when(lists.live(j))
        def _():
            out_ref[lists.group(j)] = grads_ref[j]


def place():
    here = lax.axis_index("pre")
    return lax.div(here, 2), lax.rem(here, 2), lax.axis_size("pre") // 2


def pick_kernel(capacity, lists_ref, got_ref, *out_refs):
    lists = Lists(lists_ref, capacity)
    y, core, n_y = place()
    base = lax.axis_index("table") * lax.axis_size("pre")
    for s, out_ref in enumerate(out_refs):
        chip = base + 2 * lax.rem(y + s, n_y)
        out_ref[0] = got_ref[lists.source(chip + core)]
        out_ref[1] = got_ref[lists.source(chip + 1 - core)]


def pair_kernel(*refs):
    for s, ref in enumerate(refs[:-1]):
        refs[-1][s] = ref[1]


def spread_kernel(capacity, lists_ref, got_ref, *refs):
    lists = Lists(lists_ref, capacity)
    out_ref = refs[-1]
    y, core, n_y = place()
    base = lax.axis_index("table") * lax.axis_size("pre")
    for s, ref in enumerate(refs[:-1]):
        chip = base + 2 * lax.rem(y + n_y - s, n_y)
        out_ref[lists.source(chip + core)] = ref[0]
        out_ref[lists.source(chip + 1 - core)] = got_ref[s]


def apply_kernel(lists_ref, old_ref, got_ref, copied_ref, out_ref, held, sems):
    capacity = old_ref.shape[0]
    lists = Lists(lists_ref, capacity)

    def store(j):
        return pltpu.make_async_copy(held.at[j], out_ref.at[lists.block(j)], sems.at[j])

    for j in range(capacity):
        @pl.when(lists.live(j))
        def _():
            held[j] = low(wide(old_ref[j]) - RATE * wide(got_ref[lists.group(j)]))
            store(j).start()
    for j in range(capacity):
        @pl.when(lists.live(j))
        def _():
            store(j).wait()


TILE = 128
SIDES = (0, 1)
SMALL = 0.008


def low(x):
    return x.astype(jnp.bfloat16)


def wide(x):
    return x.astype(jnp.float32)


def split(x):
    high = low(x)
    return high, low(x - wide(high))


def mm(a, b):
    return jnp.dot(a, b, preferred_element_type=jnp.float32)


def mm3(a, b):
    ah, al = a
    bh, bl = b
    return mm(ah, bh) + (mm(al, bh) + mm(ah, bl))


def total(x):
    return jnp.sum(jnp.sum(x, axis=0, keepdims=True), axis=1, keepdims=True)


def coefficients(k, mean):
    k4 = (k * k) * (k * k)
    c = 1.25 - 0.25 * (k4 * mean)
    c2 = c * c
    c3 = c2 * c
    d = c3 - 1.25 * c2
    return k4, c, c2, c3, d, 1.25 * c + c3 * d


def careful_root(x, k, mean):
    k4, c, c2, c3, d, g = coefficients(k, mean)
    xs = split(x)
    y = mm3(xs, xs) - (2.0 * k) * x
    ys = split(y)
    w = mm3(ys, ys) + (2.0 * k * k) * y
    x2 = mm3(split(w), xs) + (0.25 * mean) * w + k4 * x
    x2s = split(x2)
    y2 = mm3(x2s, x2s) - (2.0 * c) * x2
    v = c * y2 - c2 * x2 - mm3(split(y2), x2s)
    u = v - 1.25 * y2
    h = mm3(split(v), split(u)) + c3 * u + d * v - 1.25 * x2
    return k * g, k * h - g * x - mm3(xs, split(h))


def owner_kernel(
    lists_ref, got_ref, came0_ref, came1_ref, came2_ref, came3_ref, left_ref, right_ref, table_ref,
    out0_ref, out1_ref, out2_ref, out3_ref, blocks_ref, new_left_ref, new_right_ref, copied_ref,
    held, grad_ref, olds, news, x, y, e, x2, y2, xh, yh, wh, x2h, y2h, vh, uh, hh, lo, sems,
):
    fetches = [
        pltpu.make_async_copy(left_ref.at[0], olds.at[0], sems.at[0]),
        pltpu.make_async_copy(right_ref.at[0], olds.at[1], sems.at[1]),
        pltpu.make_async_copy(table_ref, held, sems.at[2]),
    ]
    stores = [
        pltpu.make_async_copy(news.at[0], new_left_ref.at[0], sems.at[3]),
        pltpu.make_async_copy(news.at[1], new_right_ref.at[0], sems.at[4]),
        pltpu.make_async_copy(held, copied_ref, sems.at[5]),
    ]
    for fetch in fetches:
        fetch.start()
    order = grad_ref.shape[0]
    piece = got_ref.shape[1]
    at_y, core, n_y = place()

    def rows(chip, core):
        return pl.ds(pl.multiple_of((2 * chip + core) * piece, piece), piece)

    for s, came_ref in enumerate((came0_ref, came1_ref, came2_ref, came3_ref)):
        chip = lax.rem(at_y + n_y - s, n_y)
        grad_ref[rows(chip, core), :] = came_ref[0]
        grad_ref[rows(chip, 1 - core), :] = got_ref[s]
    eye = lax.broadcasted_iota(jnp.int32, (TILE, TILE), 0) == lax.broadcasted_iota(
        jnp.int32, (TILE, TILE), 1
    )
    tiles = [pl.ds(at, TILE) for at in range(0, order, TILE)]

    def trace(ref):
        parts = [jnp.where(eye, ref[t, t], 0.0) for t in tiles]
        return total(functools.reduce(jnp.add, parts))

    sizes = []
    for s, contract in zip(SIDES, (1, 0)):
        gram = lax.dot_general(
            grad_ref[...], grad_ref[...], (((contract,), (contract,)), ((), ())),
            preferred_element_type=jnp.float32,
        )
        fetches[s].wait()
        new = BETA * olds[s] + (1.0 - BETA) * gram
        news[s] = new
        stores[s].start()
        sizes.append(total(new * new))
    dense = wide(grad_ref[...])
    grad_size = total(dense * dense)
    zs, means, ks, coefs = [], [], [], []
    for s in SIDES:
        diag = trace(news.at[s])
        z = 2.5 / jnp.sqrt(sizes[s] + (2.0 * EPSILON) * diag + EPSILON * EPSILON * order)
        mean = (diag + EPSILON * order) * z * (1.0 / order)
        zs.append(z)
        means.append(mean)
        ks.append(1.25 - 0.25 * mean)
        coefs.append(coefficients(ks[s], mean))
    for s in SIDES:
        scale = 0.25 * zs[s]
        scaled = news[s] * scale
        x[s] = scaled
        xh[s] = low(scaled)
        for t in tiles:
            part = news[s, t, t] * scale + jnp.where(eye, EPSILON * scale - 0.25 * means[s], 0.0)
            x[s, t, t] = part
            xh[s, t, t] = low(part)

    fourths = []
    for s in SIDES:
        square = mm(xh[s], xh[s])
        fourths.append(total(square * square))
        new = square - (2.0 * ks[s]) * x[s]
        y[s] = new
        yh[s] = low(new)
    small = jnp.sum(jnp.maximum(fourths[0], fourths[1])) <= SMALL
    for s in SIDES:
        wh[s] = low(mm(yh[s], yh[s]) + (2.0 * ks[s] * ks[s]) * y[s])
    for s in SIDES:
        k4 = coefs[s][0]
        new = mm(wh[s], xh[s]) + (0.25 * means[s]) * wide(wh[s]) + k4 * x[s]
        x2[s] = new
        x2h[s] = low(new)

    fetches[2].wait()
    stores[2].start()
    capacity = blocks_ref.shape[0]
    lists = Lists(lists_ref, capacity)
    for j in range(capacity):
        blocks_ref[j] = held[lists.block(j)]

    def finish(left_one, right_one):
        half = left_one * wide(grad_ref[...]) + (mm(vh[0], grad_ref[...]) + mm(lo[0], grad_ref[...]))
        y[0] = half
        yh[0] = low(half)
        yh[1] = low(half - wide(yh[0]))
        pre = right_one * y[0] + (mm(yh[0], vh[1]) + (mm(yh[1], vh[1]) + mm(yh[0], lo[1])))
        y[1] = pre
        scale = jnp.sqrt(jnp.sqrt(zs[0])) * jnp.sqrt(jnp.sqrt(zs[1]))
        size = scale * scale * total(pre * pre) + 1e-06
        ratio = scale * jnp.sqrt(grad_size) / jnp.sqrt(size)
        for s, out_ref in enumerate((out0_ref, out1_ref, out2_ref, out3_ref)):
            chip = lax.rem(at_y + s, n_y)
            out_ref[0] = low(y[1, rows(chip, core), :] * ratio)
            out_ref[1] = low(y[1, rows(chip, 1 - core), :] * ratio)

    @pl.when(small)
    def _():
        for s in SIDES:
            c = coefs[s][1]
            new = mm(x2h[s], x2h[s]) - (2.0 * c) * x2[s]
            y2[s] = new
            y2h[s] = low(new)
        for s in SIDES:
            _, c, c2, c3, d, _ = coefs[s]
            square, linear = y2[s], x2[s]
            cube = c * square - c2 * linear - mm(y2h[s], x2h[s])
            rest = cube - 1.25 * square
            vh[s] = low(cube)
            uh[s] = low(rest)
            e[s] = c3 * rest + d * cube - 1.25 * linear
        for s in SIDES:
            g = coefs[s][5]
            new = mm(vh[s], uh[s]) + e[s]
            hh[s] = low(new)
            e[s] = ks[s] * new - g * x[s]
        for s in SIDES:
            new = e[s] - mm(xh[s], hh[s])
            vh[s] = low(new)
            lo[s] = low(new - wide(vh[s]))
        finish(ks[0] * coefs[0][5], ks[1] * coefs[1][5])

    @pl.when(jnp.logical_not(small))
    def _():
        ones = []
        for s in SIDES:
            one, rest = careful_root(x[s], ks[s], means[s])
            ones.append(one)
            vh[s], lo[s] = split(rest)
        finish(*ones)

    for store in stores:
        store.wait()


def body(table, grads, left_stats, right_stats, block_ids, owner_slot, owner_source):
    n_table = lax.axis_size("table")
    n_pre = lax.axis_size("pre")
    capacity, piece, width = grads.shape
    order = piece * n_pre

    def shape(*dims):
        return jax.ShapeDtypeStruct(dims, jnp.bfloat16)

    n_y = n_pre // 2
    pairs = [shape(2, piece, width)] * n_y

    def along_y(sent):
        return [sent[0]] + [
            lax.ppermute(sent[s], "pre", [(i, (i + 2 * s) % n_pre) for i in range(n_pre)])
            for s in range(1, n_y)
        ]

    def across(came):
        paired = pl.pallas_call(
            pair_kernel,
            out_shape=shape(n_y, piece, width),
            in_specs=[VMEM] * n_y,
            out_specs=VMEM,
            compiler_params=params(4),
            name="pair",
        )(*came)
        return lax.ppermute(paired, "pre", [(i, i ^ 1) for i in range(n_pre)])

    lists = jnp.concatenate([owner_source, owner_slot[0], block_ids[0]])[None]
    outgoing = pl.pallas_call(
        pack_kernel,
        out_shape=shape(n_table, piece, width),
        in_specs=[SMEM, VMEM],
        out_specs=VMEM,
        compiler_params=params(4),
        name="pack",
    )(lists, grads)
    arrived = lax.all_to_all(outgoing, "table", split_axis=0, concat_axis=0, tiled=True)
    picked = pl.pallas_call(
        functools.partial(pick_kernel, capacity),
        out_shape=pairs,
        in_specs=[SMEM, VMEM],
        out_specs=[VMEM] * n_y,
        compiler_params=params(4),
        name="pick",
    )(lists, arrived)
    came = along_y(picked)
    got = across(came)
    floats = pltpu.VMEM((2, order, width), jnp.float32)
    halves = pltpu.VMEM((2, order, width), jnp.bfloat16)
    *updates, blocks, new_left, new_right, copied = pl.pallas_call(
        owner_kernel,
        out_shape=pairs + [
            shape(capacity, piece, width),
            jax.ShapeDtypeStruct(left_stats.shape, jnp.float32),
            jax.ShapeDtypeStruct(right_stats.shape, jnp.float32),
            jax.ShapeDtypeStruct(table.shape, table.dtype),
        ],
        in_specs=[SMEM] + [VMEM] * (n_y + 1) + [HBM] * 3,
        out_specs=[VMEM] * (n_y + 1) + [HBM] * 3,
        scratch_shapes=[
            pltpu.VMEM(table.shape, table.dtype),
            pltpu.VMEM((order, width), jnp.bfloat16),
        ]
        + [floats] * 7
        + [halves] * 9
        + [pltpu.SemaphoreType.DMA((6,))],
        compiler_params=params(50),
        name="owner",
    )(lists, got, *came, left_stats, right_stats, table)
    back = along_y(updates)
    got = across(back)
    spread = pl.pallas_call(
        functools.partial(spread_kernel, capacity),
        out_shape=shape(n_table, piece, width),
        in_specs=[SMEM] + [VMEM] * (n_y + 1),
        out_specs=VMEM,
        compiler_params=params(4),
        name="spread",
    )(lists, got, *back)
    home = lax.all_to_all(spread, "table", split_axis=0, concat_axis=0, tiled=True)
    new_table = pl.pallas_call(
        apply_kernel,
        out_shape=jax.ShapeDtypeStruct(table.shape, table.dtype),
        in_specs=[SMEM, VMEM, VMEM, HBM],
        out_specs=HBM,
        scratch_shapes=[
            pltpu.VMEM((capacity, piece, width), jnp.bfloat16),
            pltpu.SemaphoreType.DMA((capacity,)),
        ],
        input_output_aliases={3: 0},
        compiler_params=params(8),
        name="apply",
    )(lists, blocks, home, copied)
    return (new_table, new_left, new_right)


def solution(mesh):
    placed = (
        P("table", "pre", None),
        P("table", "pre", None),
        P(("table", "pre"), None, None),
        P(("table", "pre"), None, None),
        P("table", None),
        P("table", None),
        P(),
    )
    return jax.shard_map(
        body,
        mesh=mesh,
        in_specs=placed,
        out_specs=(
            P("table", "pre", None),
            P(("table", "pre"), None, None),
            P(("table", "pre"), None, None),
        ),
        check_vma=False,
    )
```

```python
import functools

import jax
import jax.numpy as jnp
from jax import lax
from jax.experimental import pallas as pl
from jax.experimental.pallas import tpu as pltpu
from jax.sharding import PartitionSpec as P

BETA = 0.95
EPSILON = 1.0
RATE = 0.1

VMEM = pl.BlockSpec(memory_space=pltpu.VMEM)
SMEM = pl.BlockSpec(memory_space=pltpu.SMEM)
HBM = pl.BlockSpec(memory_space=pltpu.HBM)


def params(mebibytes):
    return pltpu.CompilerParams(vmem_limit_bytes=mebibytes * 1024 * 1024)


class Lists:
    def __init__(self, ref, capacity):
        self.row, self.capacity = ref[...], capacity
        self.lanes = lax.broadcasted_iota(jnp.int32, self.row.shape, 1)
        self.total = self.row.shape[1] - 2 * capacity

    def at(self, index):
        return jnp.sum(jnp.where(self.lanes == index, self.row, 0))

    def source(self, owner):
        return self.at(owner)

    def live(self, j):
        return self.at(self.total + j) >= 0

    def group(self, j):
        return lax.div(jnp.maximum(self.at(self.total + j), 0), lax.axis_size("pre"))

    def block(self, j):
        return jnp.maximum(self.at(self.total + self.capacity + j), 0)


def pack_kernel(lists_ref, grads_ref, out_ref):
    capacity = grads_ref.shape[0]
    lists = Lists(lists_ref, capacity)
    lives = [lists.live(j) for j in range(capacity)]
    groups = [lists.group(j) for j in range(capacity)]
    for j in range(capacity):
        @pl.when(lives[j])
        def _():
            out_ref[groups[j]] = grads_ref[j]


def place():
    here = lax.axis_index("pre")
    return lax.div(here, 2), lax.rem(here, 2), lax.axis_size("pre") // 2


def pick_kernel(capacity, lists_ref, got_ref, *out_refs):
    lists = Lists(lists_ref, capacity)
    y, core, n_y = place()
    base = lax.axis_index("table") * lax.axis_size("pre")
    chips = [base + 2 * lax.rem(y + s, n_y) for s in range(n_y)]
    mine = [lists.source(chip + core) for chip in chips]
    other = [lists.source(chip + 1 - core) for chip in chips]
    for s, out_ref in enumerate(out_refs):
        out_ref[0] = got_ref[mine[s]]
        out_ref[1] = got_ref[other[s]]


def pair_kernel(*refs):
    for s, ref in enumerate(refs[:-1]):
        refs[-1][s] = ref[1]


def spread_kernel(capacity, lists_ref, got_ref, *refs):
    lists = Lists(lists_ref, capacity)
    out_ref = refs[-1]
    y, core, n_y = place()
    base = lax.axis_index("table") * lax.axis_size("pre")
    chips = [base + 2 * lax.rem(y + n_y - s, n_y) for s in range(n_y)]
    mine = [lists.source(chip + core) for chip in chips]
    other = [lists.source(chip + 1 - core) for chip in chips]
    for s, ref in enumerate(refs[:-1]):
        out_ref[mine[s]] = ref[0]
        out_ref[other[s]] = got_ref[s]


def apply_kernel(lists_ref, old_ref, got_ref, copied_ref, out_ref, held, sems):
    capacity = old_ref.shape[0]
    lists = Lists(lists_ref, capacity)

    lives = [lists.live(j) for j in range(capacity)]
    groups = [lists.group(j) for j in range(capacity)]
    blocks = [lists.block(j) for j in range(capacity)]

    def store(j):
        return pltpu.make_async_copy(held.at[j], out_ref.at[blocks[j]], sems.at[j])

    for j in range(capacity):
        @pl.when(lives[j])
        def _():
            held[j] = low(wide(old_ref[j]) - RATE * wide(got_ref[groups[j]]))
            store(j).start()
    for j in range(capacity):
        @pl.when(lives[j])
        def _():
            store(j).wait()


TILE = 128
SIDES = (0, 1)
SMALL = 0.008


def low(x):
    return x.astype(jnp.bfloat16)


def wide(x):
    return x.astype(jnp.float32)


def split(x):
    high = low(x)
    return high, low(x - wide(high))


def mm(a, b):
    return jnp.dot(a, b, preferred_element_type=jnp.float32)


def mm3(a, b):
    ah, al = a
    bh, bl = b
    return mm(ah, bh) + (mm(al, bh) + mm(ah, bl))


def total(x):
    return jnp.sum(jnp.sum(x, axis=0, keepdims=True), axis=1, keepdims=True)


def coefficients(k, mean):
    k4 = (k * k) * (k * k)
    c = 1.25 - 0.25 * (k4 * mean)
    c2 = c * c
    c3 = c2 * c
    d = c3 - 1.25 * c2
    return k4, c, c2, c3, d, 1.25 * c + c3 * d


def careful_root(x, k, mean):
    k4, c, c2, c3, d, g = coefficients(k, mean)
    xs = split(x)
    y = mm3(xs, xs) - (2.0 * k) * x
    ys = split(y)
    w = mm3(ys, ys) + (2.0 * k * k) * y
    x2 = mm3(split(w), xs) + (0.25 * mean) * w + k4 * x
    x2s = split(x2)
    y2 = mm3(x2s, x2s) - (2.0 * c) * x2
    v = c * y2 - c2 * x2 - mm3(split(y2), x2s)
    u = v - 1.25 * y2
    h = mm3(split(v), split(u)) + c3 * u + d * v - 1.25 * x2
    return k * g, k * h - g * x - mm3(xs, split(h))


def owner_kernel(
    lists_ref, got_ref, came0_ref, came1_ref, came2_ref, came3_ref, left_ref, right_ref, table_ref,
    out0_ref, out1_ref, out2_ref, out3_ref, blocks_ref, new_left_ref, new_right_ref, copied_ref,
    held, grad_ref, olds, news, d, y, e, x2, y2, dh, yh, wh, x2h, y2h, vh, uh, hh, lo, sems,
):
    fetches = [
        pltpu.make_async_copy(left_ref.at[0], olds.at[0], sems.at[0]),
        pltpu.make_async_copy(right_ref.at[0], olds.at[1], sems.at[1]),
        pltpu.make_async_copy(table_ref, held, sems.at[2]),
    ]
    stores = [
        pltpu.make_async_copy(news.at[0], new_left_ref.at[0], sems.at[3]),
        pltpu.make_async_copy(news.at[1], new_right_ref.at[0], sems.at[4]),
        pltpu.make_async_copy(held, copied_ref, sems.at[5]),
    ]
    for fetch in fetches:
        fetch.start()
    order = grad_ref.shape[0]
    piece = got_ref.shape[1]
    at_y, core, n_y = place()

    def rows(chip, core):
        return pl.ds(pl.multiple_of((2 * chip + core) * piece, piece), piece)

    for s, came_ref in enumerate((came0_ref, came1_ref, came2_ref, came3_ref)):
        chip = lax.rem(at_y + n_y - s, n_y)
        grad_ref[rows(chip, core), :] = came_ref[0]
        grad_ref[rows(chip, 1 - core), :] = got_ref[s]
    eye = lax.broadcasted_iota(jnp.int32, (TILE, TILE), 0) == lax.broadcasted_iota(
        jnp.int32, (TILE, TILE), 1
    )
    tiles = [pl.ds(at, TILE) for at in range(0, order, TILE)]
    dense = wide(grad_ref[...])
    grad_size = total(dense * dense)

    sizes, traces, mus = [], [], []
    for s, contract in zip(SIDES, (1, 0)):
        gram = lax.dot_general(
            grad_ref[...], grad_ref[...], (((contract,), (contract,)), ((), ())),
            preferred_element_type=jnp.float32,
        )
        fetches[s].wait()
        parts = [jnp.where(eye, olds[s, t, t], 0.0) for t in tiles]
        old_trace = total(functools.reduce(jnp.add, parts))
        traces.append(BETA * old_trace + (1.0 - BETA) * grad_size)
        mus.append(traces[s] * (1.0 / order))
        new = BETA * olds[s] + (1.0 - BETA) * gram
        news[s] = new
        d[s] = new
        dh[s] = low(new)
        for t in tiles:
            part = news[s, t, t] - jnp.where(eye, mus[s], 0.0)
            d[s, t, t] = part
            dh[s, t, t] = low(part)
        stores[s].start()
        sizes.append(total(new * new))
    squares = [mm(dh[s], dh[s]) for s in SIDES]

    zs, qs, means, ks, coefs = [], [], [], [], []
    for s in SIDES:
        z = 2.5 / jnp.sqrt(
            sizes[s] + (2.0 * EPSILON) * traces[s] + EPSILON * EPSILON * order
        )
        mean = (mus[s] + EPSILON) * z
        zs.append(z)
        qs.append(0.25 * z)
        means.append(mean)
        ks.append(1.25 - 0.25 * mean)
        coefs.append(coefficients(ks[s], mean))

    fourths = []
    for s in SIDES:
        square = (qs[s] * qs[s]) * squares[s]
        fourths.append(total(square * square))
        new = square - (2.0 * ks[s] * qs[s]) * d[s]
        y[s] = new
        yh[s] = low(new)
    small = jnp.sum(jnp.maximum(fourths[0], fourths[1])) <= SMALL
    for s in SIDES:
        wh[s] = low(mm(yh[s], yh[s]) + (2.0 * ks[s] * ks[s]) * y[s])
    for s in SIDES:
        k4 = coefs[s][0]
        new = (
            qs[s] * mm(wh[s], dh[s])
            + (0.25 * means[s]) * wide(wh[s])
            + (k4 * qs[s]) * d[s]
        )
        x2[s] = new
        x2h[s] = low(new)

    fetches[2].wait()
    stores[2].start()
    capacity = blocks_ref.shape[0]
    lists = Lists(lists_ref, capacity)
    for j, block in enumerate([lists.block(j) for j in range(capacity)]):
        blocks_ref[j] = held[block]

    def finish(left_one, right_one):
        half = left_one * wide(grad_ref[...]) + (mm(vh[0], grad_ref[...]) + mm(lo[0], grad_ref[...]))
        y[0] = half
        yh[0] = low(half)
        yh[1] = low(half - wide(yh[0]))
        pre = right_one * y[0] + (mm(yh[0], vh[1]) + (mm(yh[1], vh[1]) + mm(yh[0], lo[1])))
        y[1] = pre
        scale = jnp.sqrt(jnp.sqrt(zs[0])) * jnp.sqrt(jnp.sqrt(zs[1]))
        size = scale * scale * total(pre * pre) + 1e-06
        ratio = scale * jnp.sqrt(grad_size) / jnp.sqrt(size)
        for s, out_ref in enumerate((out0_ref, out1_ref, out2_ref, out3_ref)):
            chip = lax.rem(at_y + s, n_y)
            out_ref[0] = low(y[1, rows(chip, core), :] * ratio)
            out_ref[1] = low(y[1, rows(chip, 1 - core), :] * ratio)

    @pl.when(small)
    def _():
        for s in SIDES:
            c = coefs[s][1]
            new = mm(x2h[s], x2h[s]) - (2.0 * c) * x2[s]
            y2[s] = new
            y2h[s] = low(new)
        for s in SIDES:
            _, c, c2, c3, b, _ = coefs[s]
            square, linear = y2[s], x2[s]
            cube = c * square - c2 * linear - mm(y2h[s], x2h[s])
            rest = cube - 1.25 * square
            vh[s] = low(cube)
            uh[s] = low(rest)
            e[s] = c3 * rest + b * cube - 1.25 * linear
        for s in SIDES:
            g = coefs[s][5]
            new = mm(vh[s], uh[s]) + e[s]
            hh[s] = low(new)
            e[s] = ks[s] * new - (g * qs[s]) * d[s]
        for s in SIDES:
            new = e[s] - qs[s] * mm(dh[s], hh[s])
            vh[s] = low(new)
            lo[s] = low(new - wide(vh[s]))
        finish(ks[0] * coefs[0][5], ks[1] * coefs[1][5])

    @pl.when(jnp.logical_not(small))
    def _():
        ones = []
        for s in SIDES:
            one, rest = careful_root(qs[s] * d[s], ks[s], means[s])
            ones.append(one)
            vh[s], lo[s] = split(rest)
        finish(*ones)

    for store in stores:
        store.wait()


def owner_call(lists, got, *rest):
    *came, left_stats, right_stats, table = rest
    n_y, piece, width = got.shape
    order = 2 * n_y * piece
    capacity = (lists.shape[1] - lax.axis_size("table") * lax.axis_size("pre")) // 2

    def shape(*dims):
        return jax.ShapeDtypeStruct(dims, jnp.bfloat16)

    pairs = [shape(2, piece, width)] * n_y
    floats = pltpu.VMEM((2, order, width), jnp.float32)
    halves = pltpu.VMEM((2, order, width), jnp.bfloat16)
    return pl.pallas_call(
        owner_kernel,
        out_shape=pairs + [
            shape(capacity, piece, width),
            jax.ShapeDtypeStruct(left_stats.shape, jnp.float32),
            jax.ShapeDtypeStruct(right_stats.shape, jnp.float32),
            jax.ShapeDtypeStruct(table.shape, table.dtype),
        ],
        in_specs=[VMEM] * (n_y + 2) + [HBM] * 3,
        out_specs=[VMEM] * (n_y + 1) + [HBM] * 3,
        scratch_shapes=[
            pltpu.VMEM(table.shape, table.dtype),
            pltpu.VMEM((order, width), jnp.bfloat16),
        ]
        + [floats] * 7
        + [halves] * 9
        + [pltpu.SemaphoreType.DMA((6,))],
        compiler_params=params(50),
        name="owner",
    )(lists, got, *rest)


def body(table, grads, left_stats, right_stats, block_ids, owner_slot, owner_source):
    n_table = lax.axis_size("table")
    n_pre = lax.axis_size("pre")
    capacity, piece, width = grads.shape
    order = piece * n_pre

    def shape(*dims):
        return jax.ShapeDtypeStruct(dims, jnp.bfloat16)

    n_y = n_pre // 2
    pairs = [shape(2, piece, width)] * n_y

    def along_y(sent):
        return [sent[0]] + [
            lax.ppermute(sent[s], "pre", [(i, (i + 2 * s) % n_pre) for i in range(n_pre)])
            for s in range(1, n_y)
        ]

    def across(came):
        paired = pl.pallas_call(
            pair_kernel,
            out_shape=shape(n_y, piece, width),
            in_specs=[VMEM] * n_y,
            out_specs=VMEM,
            compiler_params=params(4),
            name="pair",
        )(*came)
        return lax.ppermute(paired, "pre", [(i, i ^ 1) for i in range(n_pre)])

    lists = jnp.concatenate([owner_source, owner_slot[0], block_ids[0]])[None]
    outgoing = pl.pallas_call(
        pack_kernel,
        out_shape=shape(n_table, piece, width),
        in_specs=[VMEM, VMEM],
        out_specs=VMEM,
        compiler_params=params(4),
        name="pack",
    )(lists, grads)
    arrived = lax.all_to_all(outgoing, "table", split_axis=0, concat_axis=0, tiled=True)
    picked = pl.pallas_call(
        functools.partial(pick_kernel, capacity),
        out_shape=pairs,
        in_specs=[VMEM, VMEM],
        out_specs=[VMEM] * n_y,
        compiler_params=params(4),
        name="pick",
    )(lists, arrived)
    came = along_y(picked)
    got = across(came)
    *updates, blocks, new_left, new_right, copied = owner_call(
        lists, got, *came, left_stats, right_stats, table
    )
    back = along_y(updates)
    got = across(back)
    spread = pl.pallas_call(
        functools.partial(spread_kernel, capacity),
        out_shape=shape(n_table, piece, width),
        in_specs=[VMEM] * (n_y + 2),
        out_specs=VMEM,
        compiler_params=params(4),
        name="spread",
    )(lists, got, *back)
    home = lax.all_to_all(spread, "table", split_axis=0, concat_axis=0, tiled=True)
    new_table = pl.pallas_call(
        apply_kernel,
        out_shape=jax.ShapeDtypeStruct(table.shape, table.dtype),
        in_specs=[VMEM, VMEM, VMEM, HBM],
        out_specs=HBM,
        scratch_shapes=[
            pltpu.VMEM((capacity, piece, width), jnp.bfloat16),
            pltpu.SemaphoreType.DMA((capacity,)),
        ],
        input_output_aliases={3: 0},
        compiler_params=params(8),
        name="apply",
    )(lists, blocks, home, copied)
    return (new_table, new_left, new_right)


def solution(mesh):
    placed = (
        P("table", "pre", None),
        P("table", "pre", None),
        P(("table", "pre"), None, None),
        P(("table", "pre"), None, None),
        P("table", None),
        P("table", None),
        P(),
    )
    return jax.shard_map(
        body,
        mesh=mesh,
        in_specs=placed,
        out_specs=(
            P("table", "pre", None),
            P(("table", "pre"), None, None),
            P(("table", "pre"), None, None),
        ),
        check_vma=False,
    )
```

```python
import functools

import jax
import jax.numpy as jnp
from jax import lax
from jax.experimental import pallas as pl
from jax.experimental.pallas import tpu as pltpu
from jax.sharding import PartitionSpec as P

BETA = 0.95
EPSILON = 1.0
RATE = 0.1

VMEM = pl.BlockSpec(memory_space=pltpu.VMEM)
SMEM = pl.BlockSpec(memory_space=pltpu.SMEM)
HBM = pl.BlockSpec(memory_space=pltpu.HBM)


def params(mebibytes):
    return pltpu.CompilerParams(vmem_limit_bytes=mebibytes * 1024 * 1024)


class Lists:
    def __init__(self, ref, capacity):
        self.row, self.capacity = ref[...], capacity
        self.lanes = lax.broadcasted_iota(jnp.int32, self.row.shape, 1)
        self.total = self.row.shape[1] - 2 * capacity

    def at(self, index):
        return jnp.sum(jnp.where(self.lanes == index, self.row, 0))

    def source(self, owner):
        return self.at(owner)

    def live(self, j):
        return self.at(self.total + j) >= 0

    def group(self, j):
        return lax.div(jnp.maximum(self.at(self.total + j), 0), lax.axis_size("pre"))

    def block(self, j):
        return jnp.maximum(self.at(self.total + self.capacity + j), 0)


def pack_kernel(lists_ref, grads_ref, out_ref):
    capacity = grads_ref.shape[0]
    lists = Lists(lists_ref, capacity)
    lives = [lists.live(j) for j in range(capacity)]
    groups = [lists.group(j) for j in range(capacity)]
    for j in range(capacity):
        @pl.when(lives[j])
        def _():
            out_ref[groups[j]] = grads_ref[j]


def place():
    here = lax.axis_index("pre")
    return lax.div(here, 2), lax.rem(here, 2), lax.axis_size("pre") // 2


def pick_kernel(capacity, lists_ref, got_ref, *out_refs):
    lists = Lists(lists_ref, capacity)
    y, core, n_y = place()
    base = lax.axis_index("table") * lax.axis_size("pre")
    chips = [base + 2 * lax.rem(y + s, n_y) for s in range(n_y)]
    mine = [lists.source(chip + core) for chip in chips]
    other = [lists.source(chip + 1 - core) for chip in chips]
    for s, out_ref in enumerate(out_refs):
        out_ref[0] = got_ref[mine[s]]
        out_ref[1] = got_ref[other[s]]


def pair_kernel(*refs):
    for s, ref in enumerate(refs[:-1]):
        refs[-1][s] = ref[1]


def spread_kernel(capacity, lists_ref, got_ref, *refs):
    lists = Lists(lists_ref, capacity)
    out_ref = refs[-1]
    y, core, n_y = place()
    base = lax.axis_index("table") * lax.axis_size("pre")
    chips = [base + 2 * lax.rem(y + n_y - s, n_y) for s in range(n_y)]
    mine = [lists.source(chip + core) for chip in chips]
    other = [lists.source(chip + 1 - core) for chip in chips]
    for s, ref in enumerate(refs[:-1]):
        out_ref[mine[s]] = ref[0]
        out_ref[other[s]] = got_ref[s]


def apply_kernel(lists_ref, old_ref, got_ref, copied_ref, out_ref, held, sems):
    capacity = old_ref.shape[0]
    lists = Lists(lists_ref, capacity)

    lives = [lists.live(j) for j in range(capacity)]
    groups = [lists.group(j) for j in range(capacity)]
    blocks = [lists.block(j) for j in range(capacity)]

    def store(j):
        return pltpu.make_async_copy(held.at[j], out_ref.at[blocks[j]], sems.at[j])

    for j in range(capacity):
        @pl.when(lives[j])
        def _():
            held[j] = low(wide(old_ref[j]) - RATE * wide(got_ref[groups[j]]))
            store(j).start()
    for j in range(capacity):
        @pl.when(lives[j])
        def _():
            store(j).wait()


TILE = 128
SIDES = (0, 1)
SMALL = 0.008


def low(x):
    return x.astype(jnp.bfloat16)


def wide(x):
    return x.astype(jnp.float32)


def split(x):
    high = low(x)
    return high, low(x - wide(high))


def mm(a, b):
    return jnp.dot(a, b, preferred_element_type=jnp.float32)


def mm3(a, b):
    ah, al = a
    bh, bl = b
    return mm(ah, bh) + (mm(al, bh) + mm(ah, bl))


def total(x):
    return jnp.sum(jnp.sum(x, axis=0, keepdims=True), axis=1, keepdims=True)


def coefficients(k, mean):
    k4 = (k * k) * (k * k)
    c = 1.25 - 0.25 * (k4 * mean)
    c2 = c * c
    c3 = c2 * c
    d = c3 - 1.25 * c2
    return k4, c, c2, c3, d, 1.25 * c + c3 * d


def careful_root(x, k, mean):
    k4, c, c2, c3, d, g = coefficients(k, mean)
    xs = split(x)
    y = mm3(xs, xs) - (2.0 * k) * x
    ys = split(y)
    w = mm3(ys, ys) + (2.0 * k * k) * y
    x2 = mm3(split(w), xs) + (0.25 * mean) * w + k4 * x
    x2s = split(x2)
    y2 = mm3(x2s, x2s) - (2.0 * c) * x2
    v = c * y2 - c2 * x2 - mm3(split(y2), x2s)
    u = v - 1.25 * y2
    h = mm3(split(v), split(u)) + c3 * u + d * v - 1.25 * x2
    return k * g, k * h - g * x - mm3(xs, split(h))


def owner_kernel(
    lists_ref, got_ref, came0_ref, came1_ref, came2_ref, came3_ref, left_ref, right_ref, table_ref,
    out0_ref, out1_ref, out2_ref, out3_ref, blocks_ref, new_left_ref, new_right_ref, copied_ref,
    held, grad_ref, news, d, y, e, x2, y2, dh, yh, wh, x2h, y2h, vh, uh, hh, lo, sems,
):
    fetches = [
        pltpu.make_async_copy(table_ref, held, sems.at[2]),
    ]
    stores = [
        pltpu.make_async_copy(news.at[0], new_left_ref.at[0], sems.at[3]),
        pltpu.make_async_copy(news.at[1], new_right_ref.at[0], sems.at[4]),
        pltpu.make_async_copy(held, copied_ref, sems.at[5]),
    ]
    for fetch in fetches:
        fetch.start()
    olds = (left_ref, right_ref)
    order = grad_ref.shape[0]
    piece = got_ref.shape[1]
    at_y, core, n_y = place()

    def rows(chip, core):
        return pl.ds(pl.multiple_of((2 * chip + core) * piece, piece), piece)

    lists = Lists(lists_ref, blocks_ref.shape[0])
    touched = [lists.block(j) for j in range(blocks_ref.shape[0])]
    for s, came_ref in enumerate((came0_ref, came1_ref, came2_ref, came3_ref)):
        chip = lax.rem(at_y + n_y - s, n_y)
        grad_ref[rows(chip, core), :] = came_ref[0]
        grad_ref[rows(chip, 1 - core), :] = got_ref[s]
    eye = lax.broadcasted_iota(jnp.int32, (TILE, TILE), 0) == lax.broadcasted_iota(
        jnp.int32, (TILE, TILE), 1
    )
    tiles = [pl.ds(at, TILE) for at in range(0, order, TILE)]
    dense = wide(grad_ref[...])
    grad_size = total(dense * dense)

    sizes, traces, mus = [], [], []
    for s, contract in zip(SIDES, (1, 0)):
        gram = lax.dot_general(
            grad_ref[...], grad_ref[...], (((contract,), (contract,)), ((), ())),
            preferred_element_type=jnp.float32,
        )
        parts = [jnp.where(eye, olds[s][0, t, t], 0.0) for t in tiles]
        old_trace = total(functools.reduce(jnp.add, parts))
        traces.append(BETA * old_trace + (1.0 - BETA) * grad_size)
        mus.append(traces[s] * (1.0 / order))
        new = BETA * olds[s][0] + (1.0 - BETA) * gram
        news[s] = new
        d[s] = new
        dh[s] = low(new)
        for t in tiles:
            part = news[s, t, t] - jnp.where(eye, mus[s], 0.0)
            d[s, t, t] = part
            dh[s, t, t] = low(part)
        sizes.append(total(new * new))
    squares = [mm(dh[s], dh[s]) for s in SIDES]

    zs, qs, means, ks, coefs = [], [], [], [], []
    for s in SIDES:
        z = 2.5 / jnp.sqrt(
            sizes[s] + (2.0 * EPSILON) * traces[s] + EPSILON * EPSILON * order
        )
        mean = (mus[s] + EPSILON) * z
        zs.append(z)
        qs.append(0.25 * z)
        means.append(mean)
        ks.append(1.25 - 0.25 * mean)
        coefs.append(coefficients(ks[s], mean))

    fourths = []
    for s in SIDES:
        square = (qs[s] * qs[s]) * squares[s]
        fourths.append(total(square * square))
        new = square - (2.0 * ks[s] * qs[s]) * d[s]
        y[s] = new
        yh[s] = low(new)
    small = jnp.sum(jnp.maximum(fourths[0], fourths[1])) <= SMALL
    for s in SIDES:
        wh[s] = low(mm(yh[s], yh[s]) + (2.0 * ks[s] * ks[s]) * y[s])
    for s in SIDES:
        k4 = coefs[s][0]
        new = (
            qs[s] * mm(wh[s], dh[s])
            + (0.25 * means[s]) * wide(wh[s])
            + (k4 * qs[s]) * d[s]
        )
        x2[s] = new
        x2h[s] = low(new)

    fetches[0].wait()
    for store in stores:
        store.start()

    def gather():
        for j, block in enumerate(touched):
            blocks_ref[j] = held[block]

    def finish(left_one, right_one):
        half = left_one * wide(grad_ref[...]) + (mm(vh[0], grad_ref[...]) + mm(lo[0], grad_ref[...]))
        y[0] = half
        yh[0] = low(half)
        yh[1] = low(half - wide(yh[0]))
        pre = right_one * y[0] + (mm(yh[0], vh[1]) + (mm(yh[1], vh[1]) + mm(yh[0], lo[1])))
        y[1] = pre
        scale = jnp.sqrt(jnp.sqrt(zs[0])) * jnp.sqrt(jnp.sqrt(zs[1]))
        size = scale * scale * total(pre * pre) + 1e-06
        ratio = scale * jnp.sqrt(grad_size) / jnp.sqrt(size)
        for s, out_ref in enumerate((out0_ref, out1_ref, out2_ref, out3_ref)):
            chip = lax.rem(at_y + s, n_y)
            out_ref[0] = low(y[1, rows(chip, core), :] * ratio)
            out_ref[1] = low(y[1, rows(chip, 1 - core), :] * ratio)

    @pl.when(small)
    def _():
        for s in SIDES:
            c = coefs[s][1]
            new = mm(x2h[s], x2h[s]) - (2.0 * c) * x2[s]
            y2[s] = new
            y2h[s] = low(new)
        gather()
        for s in SIDES:
            _, c, c2, c3, b, _ = coefs[s]
            square, linear = y2[s], x2[s]
            cube = c * square - c2 * linear - mm(y2h[s], x2h[s])
            rest = cube - 1.25 * square
            vh[s] = low(cube)
            uh[s] = low(rest)
            e[s] = c3 * rest + b * cube - 1.25 * linear
        for s in SIDES:
            g = coefs[s][5]
            new = mm(vh[s], uh[s]) + e[s]
            hh[s] = low(new)
            e[s] = ks[s] * new - (g * qs[s]) * d[s]
        for s in SIDES:
            new = e[s] - qs[s] * mm(dh[s], hh[s])
            vh[s] = low(new)
            lo[s] = low(new - wide(vh[s]))
        finish(ks[0] * coefs[0][5], ks[1] * coefs[1][5])

    @pl.when(jnp.logical_not(small))
    def _():
        ones = []
        for s in SIDES:
            one, rest = careful_root(qs[s] * d[s], ks[s], means[s])
            ones.append(one)
            vh[s], lo[s] = split(rest)
        gather()
        finish(*ones)

    for store in stores:
        store.wait()


def owner_call(lists, got, *rest):
    *came, left_stats, right_stats, table = rest
    n_y, piece, width = got.shape
    order = 2 * n_y * piece
    capacity = (lists.shape[1] - lax.axis_size("table") * lax.axis_size("pre")) // 2

    def shape(*dims):
        return jax.ShapeDtypeStruct(dims, jnp.bfloat16)

    pairs = [shape(2, piece, width)] * n_y
    floats = pltpu.VMEM((2, order, width), jnp.float32)
    halves = pltpu.VMEM((2, order, width), jnp.bfloat16)
    return pl.pallas_call(
        owner_kernel,
        out_shape=pairs + [
            shape(capacity, piece, width),
            jax.ShapeDtypeStruct(left_stats.shape, jnp.float32),
            jax.ShapeDtypeStruct(right_stats.shape, jnp.float32),
            jax.ShapeDtypeStruct(table.shape, table.dtype),
        ],
        in_specs=[VMEM] * (n_y + 4) + [HBM],
        out_specs=[VMEM] * (n_y + 1) + [HBM] * 3,
        scratch_shapes=[
            pltpu.VMEM(table.shape, table.dtype),
            pltpu.VMEM((order, width), jnp.bfloat16),
        ]
        + [floats] * 6
        + [halves] * 9
        + [pltpu.SemaphoreType.DMA((6,))],
        compiler_params=params(47),
        name="owner",
    )(lists, got, *rest)


def body(table, grads, left_stats, right_stats, block_ids, owner_slot, owner_source):
    n_table = lax.axis_size("table")
    n_pre = lax.axis_size("pre")
    capacity, piece, width = grads.shape
    order = piece * n_pre

    def shape(*dims):
        return jax.ShapeDtypeStruct(dims, jnp.bfloat16)

    n_y = n_pre // 2
    pairs = [shape(2, piece, width)] * n_y

    def along_y(sent):
        return [sent[0]] + [
            lax.ppermute(sent[s], "pre", [(i, (i + 2 * s) % n_pre) for i in range(n_pre)])
            for s in range(1, n_y)
        ]

    def across(came):
        paired = pl.pallas_call(
            pair_kernel,
            out_shape=shape(n_y, piece, width),
            in_specs=[VMEM] * n_y,
            out_specs=VMEM,
            compiler_params=params(4),
            name="pair",
        )(*came)
        return lax.ppermute(paired, "pre", [(i, i ^ 1) for i in range(n_pre)])

    lists = jnp.concatenate([owner_source, owner_slot[0], block_ids[0]])[None]
    outgoing = pl.pallas_call(
        pack_kernel,
        out_shape=shape(n_table, piece, width),
        in_specs=[VMEM, VMEM],
        out_specs=VMEM,
        compiler_params=params(4),
        name="pack",
    )(lists, grads)
    arrived = lax.all_to_all(outgoing, "table", split_axis=0, concat_axis=0, tiled=True)
    picked = pl.pallas_call(
        functools.partial(pick_kernel, capacity),
        out_shape=pairs,
        in_specs=[VMEM, VMEM],
        out_specs=[VMEM] * n_y,
        compiler_params=params(4),
        name="pick",
    )(lists, arrived)
    came = along_y(picked)
    got = across(came)
    *updates, blocks, new_left, new_right, copied = owner_call(
        lists, got, *came, left_stats, right_stats, table
    )
    back = along_y(updates)
    got = across(back)
    spread = pl.pallas_call(
        functools.partial(spread_kernel, capacity),
        out_shape=shape(n_table, piece, width),
        in_specs=[VMEM] * (n_y + 2),
        out_specs=VMEM,
        compiler_params=params(4),
        name="spread",
    )(lists, got, *back)
    home = lax.all_to_all(spread, "table", split_axis=0, concat_axis=0, tiled=True)
    new_table = pl.pallas_call(
        apply_kernel,
        out_shape=jax.ShapeDtypeStruct(table.shape, table.dtype),
        in_specs=[VMEM, VMEM, VMEM, HBM],
        out_specs=HBM,
        scratch_shapes=[
            pltpu.VMEM((capacity, piece, width), jnp.bfloat16),
            pltpu.SemaphoreType.DMA((capacity,)),
        ],
        input_output_aliases={3: 0},
        compiler_params=params(8),
        name="apply",
    )(lists, blocks, home, copied)
    return (new_table, new_left, new_right)


def solution(mesh):
    placed = (
        P("table", "pre", None),
        P("table", "pre", None),
        P(("table", "pre"), None, None),
        P(("table", "pre"), None, None),
        P("table", None),
        P("table", None),
        P(),
    )
    return jax.shard_map(
        body,
        mesh=mesh,
        in_specs=placed,
        out_specs=(
            P("table", "pre", None),
            P(("table", "pre"), None, None),
            P(("table", "pre"), None, None),
        ),
        check_vma=False,
    )
```
